32 devices in a mesh: seq: 8 (over y, x, core), head: 4 (over z).
Axes of the slice: x: 2, y: 2, z: 4, core: 2. Of those that a mesh axis runs over, the one named last changes fastest.
Arguments:
- tokens: bfloat16 [8192, 2048], P(('seq', 'head')), may hold values from -6 to 6
- lengths: int32 [16], replicated, may hold values from 1 to 4096, 8192 in all
- w_query: bfloat16 [2048, 2048], P(None, 'head'), may hold values from -0.125 to 0.125
- w_key: bfloat16 [2048, 2048], P(None, 'head'), may hold values from -0.125 to 0.125
- w_value: bfloat16 [2048, 2048], P(None, 'head'), may hold values from -0.125 to 0.125
- w_gate: bfloat16 [2048, 2048], P(None, 'head'), may hold values from -0.125 to 0.125
- w_forget: bfloat16 [2048, 2048], P(None, 'head'), may hold values from -0.125 to 0.125
- decay_rate: float32 [2048], P('head'), may hold values from 6.1035157e-06 to 0.04
- w_out: bfloat16 [2048, 2048], P('head'), may hold values from -0.125 to 0.125
Outputs:
- output: bfloat16 [8192, 2048], P(('seq', 'head'))
- states: float32 [8, 16, 128, 128], P('seq', 'head')
The draws below stay inside these ranges and needn't reach their ends.
Inputs may be any that keep to these rules, and one draw needn't show every extreme that they name: lengths of the prompts in stream order; they sum to 8192 and the longest is exactly 4096.
All inputs are finite; a program needn't handle non-finite values.
Results may differ from the reference program's by a relative error of at most 0.0085.
Values may be sent and summed in bfloat16 or wider, within the bound.
A program may use at most 128 MiB of HBM per device.

```python
import math
import jax
import jax.numpy as jnp
import numpy as np
from jax import lax

D = 2048
HEADS = 16
DK = 128
NDOCS = 16
TOKENS = 8192
MAXLEN = 4096
SEG = 1024
SEGS = 8


def level_of(stream_key, shape, split, smallest, high):
    loudness = 1.0
    for axis_at, parts in split:
        heights = jax.random.uniform(jax.random.fold_in(jax.random.fold_in(stream_key, 6), axis_at), (parts,), jnp.float32, smallest / len(split), high / len(split))
        loudness = loudness * jnp.repeat(jnp.exp(heights), shape[axis_at] // parts).reshape((-1,) + (1,) * (len(shape) - 1 - axis_at))
    return loudness


def length_profile(number_of, total, reach, lean):
    loads = [(1 << 20) // math.isqrt(grade ** lean) + 1 for grade in range(2, number_of + 1)]
    rest, holding = total - reach - (number_of - 1), [1] * (number_of - 1)
    while rest > 0:
        movable = [i for i in range(number_of - 1) if holding[i] < reach]
        mass, remaining = sum([loads[i] for i in movable]), rest
        for i in movable:
            extra = min(reach - holding[i], max(1, remaining * loads[i] // mass), rest)
            holding[i] = holding[i] + extra
            rest = rest - extra
    return np.array([reach] + holding)


def ragged_sizes(stream_key, number_of, total, most, slope):
    if number_of == 2:
        one = jax.random.randint(stream_key, (), max(1, total - most), min(most, total - 1) + 1)
        return jnp.stack([one, total - one])
    tallies = jnp.asarray(length_profile(number_of, total, most, slope), jnp.int32)
    twos = (number_of - 1) // 2
    source_of, receiver = tallies[1:1 + 2 * twos:2], tallies[2:2 + 2 * twos:2]
    margin = jnp.minimum(source_of - 1, most - receiver)
    shifted = jax.random.randint(jax.random.fold_in(stream_key, 1), (twos,), 0, 1 << 20) % (margin + 1)
    tallies = tallies.at[1:1 + 2 * twos:2].set(source_of - shifted).at[2:2 + 2 * twos:2].set(receiver + shifted)
    return tallies[jax.random.permutation(jax.random.fold_in(stream_key, 2), number_of)]


def scatter_about(key, dims, scale, most, split=(), kind=jnp.bfloat16):
    values = scale * jax.random.normal(key, dims, jnp.float32)
    if split:
        values = values * level_of(key, dims, split, -0.22, 0.18)
    return jnp.clip(values, -most, most).astype(kind)


def setup_inputs(seed: int = 0) -> dict:
    seeds = jax.random.split(jax.random.key(seed), 10)
    return {
        "tokens": scatter_about(seeds[0], (TOKENS, D), 1.0, 6.0, ((0, 32),)),
        "lengths": ragged_sizes(seeds[1], NDOCS, TOKENS, MAXLEN, 2).astype(jnp.int32),
        "w_query": scatter_about(seeds[2], (D, D), D ** -0.5, 0.125, ((1, 4),)),
        "w_key": scatter_about(seeds[3], (D, D), D ** -0.5, 0.125, ((1, 4),)),
        "w_value": scatter_about(seeds[4], (D, D), D ** -0.5, 0.125, ((1, 4),)),
        "w_gate": scatter_about(seeds[5], (D, D), D ** -0.5, 0.125, ((1, 4),)),
        "w_forget": scatter_about(seeds[6], (D, D), D ** -0.5, 0.125, ((1, 4),)),
        "decay_rate": jnp.clip(jnp.exp(math.log(0.04) - 8.78776976 * jax.random.uniform(seeds[7], (D,), jnp.float32) ** level_of(seeds[7], (D,), ((0, 4),), -0.2, 0.2)), 6.10351571594947e-06, 0.04),
        "w_out": scatter_about(seeds[8], (D, D), D ** -0.5, 0.125, ((0, 4),)),
    }


def reference(tokens, lengths, w_query, w_key, w_value, w_gate, w_forget, decay_rate, w_out):
    tokens_f = tokens.astype(jnp.float32)
    normed = (tokens_f * lax.rsqrt(lax.optimization_barrier(jnp.mean(tokens_f * tokens_f, axis=-1, keepdims=True)) + 1e-05)).astype(jnp.bfloat16)
    queries = jnp.dot(normed, w_query, preferred_element_type=jnp.float32).astype(jnp.bfloat16)
    key_rows = jnp.dot(normed, w_key, preferred_element_type=jnp.float32).astype(jnp.bfloat16)
    value_rows = jnp.dot(normed, w_value, preferred_element_type=jnp.float32).astype(jnp.bfloat16)
    gate_rows = jnp.dot(normed, w_gate, preferred_element_type=jnp.float32).astype(jnp.bfloat16)
    queries, key_rows, value_rows, gate_rows = lax.optimization_barrier((queries, key_rows, value_rows, gate_rows))
    forget_logit = jnp.dot(normed, w_forget, preferred_element_type=jnp.float32)
    log_decay = -decay_rate.astype(jnp.float32)[None, :] * jax.nn.softplus(forget_logit)
    doc_ends = jnp.cumsum(lengths).astype(jnp.int32)
    starts = (doc_ends - lengths).astype(jnp.int32)
    positions = jnp.arange(TOKENS, dtype=jnp.int32)
    doc_ids = lax.optimization_barrier(jnp.sum((starts[None, :] <= positions[:, None]).astype(jnp.int32), axis=1)) - 1
    prev_doc = jnp.concatenate([jnp.full((1,), -1, jnp.int32), doc_ids[:-1].astype(jnp.int32)])
    keep_prev = (doc_ids == prev_doc).astype(jnp.float32)
    factor = jnp.exp(log_decay) * keep_prev[:, None]
    seg_shape = (SEGS, SEG, HEADS, DK)
    per_segment = (queries.astype(jnp.float32).reshape(seg_shape), key_rows.astype(jnp.float32).reshape(seg_shape), value_rows.astype(jnp.float32).reshape(seg_shape), factor.reshape(seg_shape))

    def advance(held_state, token_row):
        held_state = held_state * token_row[3][:, :, None] + token_row[1][:, :, None] * token_row[2][:, None, :]
        return (held_state, lax.optimization_barrier(jnp.sum(token_row[0][:, :, None] * held_state, axis=1)))

    def segment(held_state, seg_block):
        held_state, seg_outs = lax.scan(advance, held_state, seg_block)
        return (held_state, (seg_outs, held_state))
    _, (mixed, states) = lax.scan(segment, jnp.zeros((HEADS, DK, DK), jnp.float32), per_segment)
    mixed = mixed.reshape(TOKENS, HEADS, DK)
    inverse = lax.rsqrt(lax.optimization_barrier(jnp.mean(mixed * mixed, axis=-1, keepdims=True)) + 1e-05)
    gate_f = jax.nn.silu(gate_rows.astype(jnp.float32)).reshape(TOKENS, HEADS, DK)
    gated = (mixed * inverse * gate_f).astype(jnp.bfloat16).reshape(TOKENS, D)
    output = (tokens_f + jnp.dot(gated, w_out, preferred_element_type=jnp.float32)).astype(jnp.bfloat16)
    return (output, states)
```

```python
import functools

import jax
import jax.numpy as jnp
from jax import lax
from jax.experimental import pallas as pl
from jax.experimental.pallas import tpu as pltpu
from jax.sharding import PartitionSpec as P

DK = 128
MESH = pl.DeviceIdType.MESH
NT = (((1,), (1,)), ((), ()))
TN = (((0,), (0,)), ((), ()))
F32, BF16 = jnp.float32, jnp.bfloat16


def dot(a, b, dims=(((1,), (0,)), ((), ()))):
    return lax.dot_general(a, b, dims, preferred_element_type=F32)


def block_by_distance(i, z, n):
    up = jnp.where(2 * z < n, 1, -1)
    near = jnp.where(2 * z < n, z, n - 1 - z)
    half = (i + 1) // 2
    paired = jnp.where(i % 2 == 1, z + up * half, z - up * half)
    single = jnp.where(2 * z < n, i, n - 1 - i)
    return jnp.where(i <= 2 * near, paired, single)


def project_kernel(
    n, tokens_ref, rate_ref, doc_col, doc_row, prev_ref, wq, wk, wv, wg, wf,
    local_ref, cq_ref, gate_ref, state_ref, decay_ref,
    gathered, weights, load_sem, send_sem, recv_sem,
):
    z = lax.axis_index("head")
    loads = [
        pltpu.make_async_copy(w, weights.at[i], load_sem.at[i])
        for i, w in enumerate((wf, wq, wk, wv, wg))
    ]
    for load in loads:
        load.start()

    barrier = pltpu.get_barrier_semaphore()

    @pl.when(z > 0)
    def _():
        pl.semaphore_signal(barrier, inc=1, device_id={"head": z - 1}, device_id_type=MESH)

    @pl.when(z < n - 1)
    def _():
        pl.semaphore_signal(barrier, inc=1, device_id={"head": z + 1}, device_id_type=MESH)

    tokens = tokens_ref[...].astype(F32)
    scale = lax.rsqrt(jnp.mean(tokens * tokens, axis=-1, keepdims=True) + 1e-05)
    gathered[z] = (tokens * scale).astype(BF16)

    peers = jnp.where(z > 0, 1, 0) + jnp.where(z < n - 1, 1, 0)
    pl.semaphore_wait(barrier, peers)

    def pass_on(b, way):
        return pltpu.make_async_remote_copy(
            src_ref=gathered.at[b],
            dst_ref=gathered.at[b],
            send_sem=send_sem.at[(way + 1) // 2, b],
            recv_sem=recv_sem.at[b],
            device_id={"head": z + way},
            device_id_type=MESH,
        )

    rows = tokens_ref.shape[0]
    half = rows // 2
    width = rate_ref.shape[1]
    row_at = lax.broadcasted_iota(jnp.int32, (rows, rows), 0)
    col_at = lax.broadcasted_iota(jnp.int32, (rows, rows), 1)
    lower = row_at >= col_at
    lower_bf = lower.astype(F32).astype(BF16)

    def step(i, carry):
        b = block_by_distance(i, z, n)

        @pl.when(i > 0)
        def _():
            pltpu.make_async_remote_copy(
                src_ref=gathered.at[b],
                dst_ref=gathered.at[b],
                send_sem=send_sem.at[0, b],
                recv_sem=recv_sem.at[b],
                device_id={"head": z},
                device_id_type=MESH,
            ).wait_recv()

        @pl.when((b <= z) & (z < n - 1))
        def _():
            pass_on(b, 1).start()

        @pl.when((b >= z) & (z > 0))
        def _():
            pass_on(b, -1).start()

        @pl.when(i == 0)
        def _():
            for load in loads:
                load.wait()

        x = gathered[b]
        logit = dot(x, weights[0])
        softplus = jnp.maximum(logit, 0.0) + jnp.log1p(jnp.exp(-jnp.abs(logit)))
        log_decay = -rate_ref[...] * softplus
        high = log_decay.astype(BF16)
        low = (log_decay - high.astype(F32)).astype(BF16)
        cum = dot(lower_bf, high) + dot(lower_bf, low)
        q = dot(x, weights[1]).astype(BF16).astype(F32)
        k = dot(x, weights[2]).astype(BF16).astype(F32)
        v = dot(x, weights[3]).astype(BF16)
        gate_ref[b] = dot(x, weights[4]).astype(BF16)

        docs = doc_col[b]
        same = lower & (docs == doc_row[b])
        last_doc = docs[rows - 1 :, :]
        prev = prev_ref[b]
        carried = (docs == prev).astype(F32)
        ending = (docs == last_doc).astype(F32)
        keep = (last_doc == prev).astype(F32)
        last = cum[rows - 1 :, :]
        middle = cum[half - 1 : half, :]
        decay_ref[b] = jnp.exp(last) * keep
        cq_ref[b] = (q * jnp.exp(cum) * carried).astype(BF16)
        k_end = (k * jnp.exp(last - cum) * ending).astype(BF16)
        top, low_half = slice(0, half), slice(half, rows)
        top_mid, low_mid = 0.5 * middle, 0.5 * (middle + last)
        q_top = (q[top] * jnp.exp(cum[top] - top_mid)).astype(BF16)
        k_top = (k[top] * jnp.exp(top_mid - cum[top])).astype(BF16)
        q_low = (q[low_half] * jnp.exp(cum[low_half] - low_mid)).astype(BF16)
        k_low = (k[low_half] * jnp.exp(low_mid - cum[low_half])).astype(BF16)
        q_cross = (q[low_half] * jnp.exp(cum[low_half] - middle)).astype(BF16)
        k_cross = (k[top] * jnp.exp(middle - cum[top])).astype(BF16)
        for h in range(width // DK):
            c = slice(h * DK, (h + 1) * DK)
            s_top = jnp.where(same[top, top], dot(q_top[:, c], k_top[:, c], NT), 0.0)
            s_cross = jnp.where(same[low_half, top], dot(q_cross[:, c], k_cross[:, c], NT), 0.0)
            s_low = jnp.where(
                same[low_half, low_half], dot(q_low[:, c], k_low[:, c], NT), 0.0
            )
            local_ref[b, top, c] = dot(s_top.astype(BF16), v[top, c])
            s_both = jnp.concatenate([s_cross, s_low], axis=1).astype(BF16)
            local_ref[b, low_half, c] = dot(s_both, v[:, c])
            state_ref[b, h] = dot(v[:, c], k_end[:, c], TN)
        return carry

    lax.fori_loop(0, n, step, 0)

    def finish(i, carry):
        @pl.when((i <= z) & (z < n - 1))
        def _():
            pass_on(i, 1).wait_send()

        @pl.when((i >= z) & (z > 0))
        def _():
            pass_on(i, -1).wait_send()

        return carry

    lax.fori_loop(0, n, finish, 0)


def output_kernel(
    n, tokens_ref, local_ref, cq_ref, gate_ref, state_ref, w_ref, out_ref,
    sending, arrived, weights, load_sem, send_sem, recv_sem,
):
    z = lax.axis_index("head")
    load = pltpu.make_async_copy(w_ref, weights, load_sem)
    load.start()
    barrier = pltpu.get_barrier_semaphore()
    for away in range(1, n):
        pl.semaphore_signal(
            barrier, inc=1, device_id={"head": (z + away) % n}, device_id_type=MESH
        )
    pl.semaphore_wait(barrier, n - 1)
    width = cq_ref.shape[2]

    def send(b):
        return pltpu.make_async_remote_copy(
            src_ref=sending.at[b],
            dst_ref=arrived.at[z],
            send_sem=send_sem.at[b],
            recv_sem=recv_sem.at[z],
            device_id={"head": b},
            device_id_type=MESH,
        )

    def gated(i, carry):
        b = block_by_distance(n - 1 - i, z, n)
        for h in range(width // DK):
            c = slice(h * DK, (h + 1) * DK)
            mixed = local_ref[b, :, c] + dot(cq_ref[b, :, c], state_ref[b, h], NT)
            inverse = lax.rsqrt(jnp.mean(mixed * mixed, axis=-1, keepdims=True) + 1e-05)
            gate = gate_ref[b, :, c].astype(F32)
            sending[b, :, c] = (mixed * inverse * (gate * jax.nn.sigmoid(gate))).astype(BF16)

        @pl.when(i < n - 1)
        def _():
            send(b).start()

        return carry

    lax.fori_loop(0, n, gated, 0)
    load.wait()
    out = tokens_ref[...].astype(F32) + dot(sending[z], weights[z])
    for away in range(1, n):
        b = block_by_distance(away, z, n)
        pltpu.make_async_remote_copy(
            src_ref=sending.at[b],
            dst_ref=arrived.at[b],
            send_sem=send_sem.at[b],
            recv_sem=recv_sem.at[b],
            device_id={"head": b},
            device_id_type=MESH,
        ).wait_recv()
        out = out + dot(arrived[b], weights[b])
    out_ref[...] = out.astype(BF16)
    for away in range(1, n):
        send((z + away) % n).wait_send()


def local(tokens, lengths, w_query, w_key, w_value, w_gate, w_forget, decay_rate, w_out):
    n, segs = lax.axis_size("head"), lax.axis_size("seq")
    seq = lax.axis_index("seq")
    rows, features = tokens.shape
    width = w_query.shape[1]
    heads = width // DK
    seg_len = rows * n

    piece_rows = width // segs
    own_piece = lax.dynamic_slice_in_dim(w_out, seq * piece_rows, piece_rows, 0)
    w_full = lax.all_gather(own_piece, ("head", "seq"), axis=0, tiled=True)
    w_full = w_full.reshape(n, width, features)

    docs_at = jnp.arange(lengths.shape[0])
    starts = jnp.sum(jnp.where(docs_at[None, :] < docs_at[:, None], lengths[None, :], 0), axis=1)
    positions = seq * seg_len - 1 + jnp.arange(seg_len + 1, dtype=jnp.int32)
    doc_ids = jnp.sum((starts[None, :] <= positions[:, None]).astype(jnp.int32), axis=1) - 1
    own_docs = doc_ids[1:].reshape(n, rows)
    prev = doc_ids[:-1].reshape(n, rows)[:, :1].reshape(n, 1, 1)

    vmem, anywhere = pl.BlockSpec(memory_space=pltpu.VMEM), pl.BlockSpec(memory_space=pl.ANY)
    shape = jax.ShapeDtypeStruct
    within, carried_q, gates, block_state, block_decay = pl.pallas_call(
        functools.partial(project_kernel, n),
        out_shape=(
            shape((n, rows, width), F32),
            shape((n, rows, width), BF16),
            shape((n, rows, width), BF16),
            shape((n, heads, DK, DK), F32),
            shape((n, 1, width), F32),
        ),
        in_specs=[vmem] * 5 + [anywhere] * 5,
        out_specs=(vmem,) * 5,
        scratch_shapes=[
            pltpu.VMEM((n, rows, features), BF16),
            pltpu.VMEM((5, features, width), BF16),
            pltpu.SemaphoreType.DMA((5,)),
            pltpu.SemaphoreType.DMA((2, n)),
            pltpu.SemaphoreType.DMA((n,)),
        ],
        compiler_params=pltpu.CompilerParams(
            collective_id=0, has_side_effects=True, vmem_limit_bytes=50 * 2**20
        ),
        cost_estimate=pl.CostEstimate(
            flops=80 * seg_len * features * width, bytes_accessed=12 * features * width, transcendentals=0
        ),
        name="project",
    )(
        tokens, decay_rate[None, :], own_docs[:, :, None], own_docs[:, None, :], prev,
        w_query, w_key, w_value, w_gate, w_forget,
    )

    block_state, block_decay, w_full = lax.optimization_barrier((block_state, block_decay, w_full))
    decays = block_decay.reshape(n, heads, 1, DK)
    seg_state, seg_decay = block_state[0], decays[0]
    for b in range(1, n):
        seg_state = seg_state * decays[b] + block_state[b]
        seg_decay = seg_decay * decays[b]
    high = seg_decay.astype(BF16)
    rest = seg_decay - high.astype(F32)
    low = rest.astype(BF16)
    packet = jnp.concatenate(
        [seg_state.astype(BF16), high, low, jnp.zeros((heads, 14, DK), BF16)], axis=1
    )
    packets = lax.all_gather(packet, "seq", axis=0, tiled=False).astype(F32)
    incoming = jnp.zeros((heads, DK, DK), F32)
    for j in range(segs - 1):
        decay_j = packets[j, :, DK : DK + 1] + packets[j, :, DK + 1 : DK + 2]
        incoming = jnp.where(j < seq, incoming * decay_j + packets[j, :, :DK], incoming)
    end_state = jnp.swapaxes(seg_decay * incoming + seg_state, 1, 2)
    entering = [incoming]
    for b in range(n - 1):
        entering.append(entering[-1] * decays[b] + block_state[b])
    entering = jnp.stack(entering).astype(BF16)

    output = pl.pallas_call(
        functools.partial(output_kernel, n),
        out_shape=shape((rows, features), BF16),
        in_specs=[vmem] * 5 + [anywhere],
        out_specs=vmem,
        scratch_shapes=[
            pltpu.VMEM((n, rows, width), BF16),
            pltpu.VMEM((n, rows, width), BF16),
            pltpu.VMEM((n, width, features), BF16),
            pltpu.SemaphoreType.DMA,
            pltpu.SemaphoreType.DMA((n,)),
            pltpu.SemaphoreType.DMA((n,)),
        ],
        compiler_params=pltpu.CompilerParams(
            collective_id=1, has_side_effects=True, vmem_limit_bytes=50 * 2**20
        ),
        cost_estimate=pl.CostEstimate(
            flops=2 * rows * n * width * features, bytes_accessed=8 * features * width, transcendentals=0
        ),
        name="mix_out",
    )(tokens, within, carried_q, gates, entering, w_full)
    return (output, end_state[None])


def solution(mesh):
    in_specs = (
        P(("seq", "head"), None),
        P(),
        P(None, "head"),
        P(None, "head"),
        P(None, "head"),
        P(None, "head"),
        P(None, "head"),
        P("head"),
        P("head", None),
    )
    out_specs = (P(("seq", "head"), None), P("seq", "head", None, None))
    return jax.shard_map(local, mesh=mesh, in_specs=in_specs, out_specs=out_specs, check_vma=False)
```

```python
import functools

import jax
import jax.numpy as jnp
from jax import lax
from jax.experimental import pallas as pl
from jax.experimental.pallas import tpu as pltpu
from jax.sharding import PartitionSpec as P

DK = 128
MESH = pl.DeviceIdType.MESH
NT = (((1,), (1,)), ((), ()))
TN = (((0,), (0,)), ((), ()))
F32, BF16 = jnp.float32, jnp.bfloat16


def dot(a, b, dims=(((1,), (0,)), ((), ()))):
    return lax.dot_general(a, b, dims, preferred_element_type=F32)


def block_by_distance(i, z, n):
    up = jnp.where(2 * z < n, 1, -1)
    near = jnp.where(2 * z < n, z, n - 1 - z)
    half = (i + 1) // 2
    paired = jnp.where(i % 2 == 1, z + up * half, z - up * half)
    single = jnp.where(2 * z < n, i, n - 1 - i)
    return jnp.where(i <= 2 * near, paired, single)


def layer_kernel(
    n, segs, tokens_ref, rate_ref, doc_col, doc_row, prev_ref, piece_ref, wq, wk, wv, wg, wf,
    out_ref, end_ref,
    gathered, weights, w_all, local_ref, cq_ref, gate_ref, state_ref, decay_ref,
    packets, seg_state, incoming, entering, sending, arrived,
    load_sem, send_sem, recv_sem, wz_send, wz_recv, wp_send, wp_recv, wc_send, wc_recv,
    state_send, state_recv, mix_send, mix_recv,
):
    z, seq = lax.axis_index("head"), lax.axis_index("seq")
    chips = segs // 2
    chip, core = seq // 2, seq % 2
    rows, features = tokens_ref.shape
    half = rows // 2
    width = rate_ref.shape[1]
    heads = width // DK
    loads = [
        pltpu.make_async_copy(w, weights.at[i], load_sem.at[i])
        for i, w in enumerate((wf, wq, wk, wv, wg))
    ]
    for load in loads:
        load.start()

    barrier = pltpu.get_barrier_semaphore()

    def greet_seq(away, carry):
        pl.semaphore_signal(
            barrier, inc=1, device_id={"seq": (seq + away) % segs}, device_id_type=MESH
        )
        return carry

    def greet_head(away, carry):
        pl.semaphore_signal(
            barrier, inc=1, device_id={"head": (z + away) % n}, device_id_type=MESH
        )
        return carry

    lax.fori_loop(1, segs, greet_seq, 0)
    lax.fori_loop(1, n, greet_head, 0)

    tokens = tokens_ref[...].astype(F32)
    scale = lax.rsqrt(jnp.mean(tokens * tokens, axis=-1, keepdims=True) + 1e-05)
    gathered[z] = (tokens * scale).astype(BF16)
    w_all[z, core, chip] = piece_ref[...]
    pl.semaphore_wait(barrier, segs - 1 + n - 1)

    def pass_tokens(b, way):
        return pltpu.make_async_remote_copy(
            src_ref=gathered.at[b],
            dst_ref=gathered.at[b],
            send_sem=send_sem.at[(way + 1) // 2, b],
            recv_sem=recv_sem.at[b],
            device_id={"head": (z + way + n) % n},
            device_id_type=MESH,
        )

    def pass_piece(b, way):
        return pltpu.make_async_remote_copy(
            src_ref=w_all.at[b, core, chip],
            dst_ref=w_all.at[b, core, chip],
            send_sem=wz_send.at[(way + 1) // 2, b],
            recv_sem=wz_recv.at[b],
            device_id={"head": (z + way + n) % n},
            device_id_type=MESH,
        )

    def spread_piece(b, source, target):
        return pltpu.make_async_remote_copy(
            src_ref=w_all.at[b, core, source],
            dst_ref=w_all.at[b, core, source],
            send_sem=wp_send.at[b, target],
            recv_sem=wp_recv.at[b, source],
            device_id={"seq": 2 * target + core},
            device_id_type=MESH,
        )

    def share_pieces(b, from_core):
        return pltpu.make_async_remote_copy(
            src_ref=w_all.at[b, from_core],
            dst_ref=w_all.at[b, from_core],
            send_sem=wc_send.at[b],
            recv_sem=wc_recv.at[b],
            device_id={"seq": 2 * chip + 1 - core},
            device_id_type=MESH,
        )

    def both_ways(b, copy, act):
        @pl.when((b <= z) & (z < n - 1))
        def _():
            act(copy(b, 1))

        @pl.when((b >= z) & (z > 0))
        def _():
            act(copy(b, -1))

    def start(copy):
        copy.start()

    def wait_send(copy):
        copy.wait_send()

    def share_after_spread(b):
        def arrival(away, carry):
            spread_piece(b, (chip + away) % chips, (chip + away) % chips).wait_recv()
            return carry

        lax.fori_loop(1, chips, arrival, 0)
        share_pieces(b, core).start()

    row_at = lax.broadcasted_iota(jnp.int32, (rows, rows), 0)
    col_at = lax.broadcasted_iota(jnp.int32, (rows, rows), 1)
    lower = row_at >= col_at
    lower_bf = lower.astype(F32).astype(BF16)

    def step(i, carry):
        b = block_by_distance(i, z, n)

        @pl.when(i > 0)
        def _():
            pass_piece(b, 1).wait_recv()

        both_ways(b, pass_piece, start)

        @pl.when(i > 0)
        def _():
            pass_tokens(b, 1).wait_recv()

        both_ways(b, pass_tokens, start)

        def spread(away, inner):
            spread_piece(b, chip, (chip + away) % chips).start()
            return inner

        lax.fori_loop(1, chips, spread, 0)

        @pl.when(i > 0)
        def _():
            share_after_spread(block_by_distance(i - 1, z, n))

        @pl.when(i == 0)
        def _():
            for load in loads:
                load.wait()

        x = gathered[b]
        logit = dot(x, weights[0])
        softplus = jnp.maximum(logit, 0.0) + jnp.log1p(jnp.exp(-jnp.abs(logit)))
        log_decay = -rate_ref[...] * softplus
        high = log_decay.astype(BF16)
        low = (log_decay - high.astype(F32)).astype(BF16)
        cum = dot(lower_bf, high) + dot(lower_bf, low)
        q = dot(x, weights[1]).astype(BF16).astype(F32)
        k = dot(x, weights[2]).astype(BF16).astype(F32)
        v = dot(x, weights[3]).astype(BF16)
        gate_ref[b] = dot(x, weights[4]).astype(BF16)

        docs = doc_col[b]
        same = lower & (docs == doc_row[b])
        last_doc = docs[rows - 1 :, :]
        prev = prev_ref[b]
        carried = (docs == prev).astype(F32)
        ending = (docs == last_doc).astype(F32)
        keep = (last_doc == prev).astype(F32)
        last = cum[rows - 1 :, :]
        middle = cum[half - 1 : half, :]
        decay_ref[b] = jnp.exp(last) * keep
        cq_ref[b] = (q * jnp.exp(cum) * carried).astype(BF16)
        k_end = (k * jnp.exp(last - cum) * ending).astype(BF16)
        top, low_half = slice(0, half), slice(half, rows)
        top_mid, low_mid = 0.5 * middle, 0.5 * (middle + last)
        q_top = (q[top] * jnp.exp(cum[top] - top_mid)).astype(BF16)
        k_top = (k[top] * jnp.exp(top_mid - cum[top])).astype(BF16)
        q_low = (q[low_half] * jnp.exp(cum[low_half] - low_mid)).astype(BF16)
        k_low = (k[low_half] * jnp.exp(low_mid - cum[low_half])).astype(BF16)
        q_cross = (q[low_half] * jnp.exp(cum[low_half] - middle)).astype(BF16)
        k_cross = (k[top] * jnp.exp(middle - cum[top])).astype(BF16)
        for h in range(width // DK):
            c = slice(h * DK, (h + 1) * DK)
            s_top = jnp.where(same[top, top], dot(q_top[:, c], k_top[:, c], NT), 0.0)
            s_cross = jnp.where(same[low_half, top], dot(q_cross[:, c], k_cross[:, c], NT), 0.0)
            s_low = jnp.where(
                same[low_half, low_half], dot(q_low[:, c], k_low[:, c], NT), 0.0
            )
            local_ref[b, top, c] = dot(s_top.astype(BF16), v[top, c])
            s_both = jnp.concatenate([s_cross, s_low], axis=1).astype(BF16)
            local_ref[b, low_half, c] = dot(s_both, v[:, c])
            state_ref[b, h] = dot(v[:, c], k_end[:, c], TN)
        return carry

    lax.fori_loop(0, n, step, 0)

    def send_state(to):
        return pltpu.make_async_remote_copy(
            src_ref=packets.at[seq],
            dst_ref=packets.at[seq],
            send_sem=state_send.at[to],
            recv_sem=state_recv.at[seq],
            device_id={"seq": to},
            device_id_type=MESH,
        )

    seg_decay = decay_ref[0]
    for b in range(1, n):
        seg_decay = seg_decay * decay_ref[b]
    high = seg_decay.astype(BF16).astype(F32)
    low = seg_decay - high
    pad_at = lax.broadcasted_iota(jnp.int32, (16, DK), 0)
    for h in range(heads):
        c = slice(h * DK, (h + 1) * DK)
        total = state_ref[0, h]
        for b in range(1, n):
            total = total * decay_ref[b][:, c] + state_ref[b, h]
        seg_state[h] = total
        packets[seq, h, :DK] = total.astype(BF16)
        pad = jnp.where(pad_at == 0, high[:, c], jnp.where(pad_at == 1, low[:, c], 0.0))
        packets[seq, h, DK:] = pad.astype(BF16)

    def send_later(away, carry):
        @pl.when(seq + away < segs)
        def _():
            send_state(seq + away).start()

        return carry

    lax.fori_loop(1, segs, send_later, 0)
    share_after_spread(block_by_distance(n - 1, z, n))

    incoming[...] = jnp.zeros_like(incoming)

    def take(j, carry):
        @pl.when(j < seq)
        def _():
            pltpu.make_async_remote_copy(
                src_ref=packets.at[j],
                dst_ref=packets.at[j],
                send_sem=state_send.at[j],
                recv_sem=state_recv.at[j],
                device_id={"seq": (seq + 1) % segs},
                device_id_type=MESH,
            ).wait_recv()
            for h in range(heads):
                pad = packets[j, h, DK:].astype(F32)
                decay = pad[0:1] + pad[1:2]
                incoming[h] = incoming[h] * decay + packets[j, h, :DK].astype(F32)

        return carry

    lax.fori_loop(0, segs - 1, take, 0)
    for h in range(heads):
        c = slice(h * DK, (h + 1) * DK)
        held = incoming[h]
        end_ref[h] = (held * seg_decay[:, c] + seg_state[h]).T
        for b in range(n):
            entering[b, h] = held.astype(BF16)
            if b < n - 1:
                held = held * decay_ref[b][:, c] + state_ref[b, h]

    def send_mix(b):
        return pltpu.make_async_remote_copy(
            src_ref=sending.at[b],
            dst_ref=arrived.at[z],
            send_sem=mix_send.at[b],
            recv_sem=mix_recv.at[z],
            device_id={"head": b},
            device_id_type=MESH,
        )

    def gated(i, carry):
        b = block_by_distance(n - 1 - i, z, n)
        for h in range(heads):
            c = slice(h * DK, (h + 1) * DK)
            mixed = local_ref[b, :, c] + dot(cq_ref[b, :, c], entering[b, h], NT)
            inverse = lax.rsqrt(jnp.mean(mixed * mixed, axis=-1, keepdims=True) + 1e-05)
            gate = gate_ref[b, :, c].astype(F32)
            sending[b, :, c] = (mixed * inverse * (gate * jax.nn.sigmoid(gate))).astype(BF16)

        @pl.when(i < n - 1)
        def _():
            send_mix(b).start()

        return carry

    lax.fori_loop(0, n, gated, 0)

    def whole(b):
        share_pieces(b, 1 - core).wait_recv()
        return w_all[b].reshape(width, features)

    out = tokens_ref[...].astype(F32) + dot(sending[z], whole(z))
    for away in range(1, n):
        b = block_by_distance(away, z, n)
        w_b = whole(b)
        pltpu.make_async_remote_copy(
            src_ref=sending.at[b],
            dst_ref=arrived.at[b],
            send_sem=mix_send.at[b],
            recv_sem=mix_recv.at[b],
            device_id={"head": b},
            device_id_type=MESH,
        ).wait_recv()
        out = out + dot(arrived[b], w_b)
    out_ref[...] = out.astype(BF16)

    def finish(b, carry):
        both_ways(b, pass_tokens, wait_send)
        both_ways(b, pass_piece, wait_send)
        share_pieces(b, core).wait_send()

        def spread_done(away, inner):
            spread_piece(b, chip, (chip + away) % chips).wait_send()
            return inner

        lax.fori_loop(1, chips, spread_done, 0)

        @pl.when(b != z)
        def _():
            send_mix(b).wait_send()

        return carry

    lax.fori_loop(0, n, finish, 0)

    def later_done(away, carry):
        @pl.when(seq + away < segs)
        def _():
            send_state(seq + away).wait_send()

        return carry

    lax.fori_loop(1, segs, later_done, 0)


def local(tokens, lengths, w_query, w_key, w_value, w_gate, w_forget, decay_rate, w_out):
    n, segs = lax.axis_size("head"), lax.axis_size("seq")
    seq = lax.axis_index("seq")
    rows, features = tokens.shape
    width = w_query.shape[1]
    heads = width // DK
    seg_len = rows * n
    chips = segs // 2

    piece_rows = width // segs
    piece_at = ((seq % 2) * chips + seq // 2) * piece_rows
    own_piece = lax.dynamic_slice_in_dim(w_out, piece_at, piece_rows, 0)

    docs_at = jnp.arange(lengths.shape[0])
    starts = jnp.sum(jnp.where(docs_at[None, :] < docs_at[:, None], lengths[None, :], 0), axis=1)
    positions = seq * seg_len - 1 + jnp.arange(seg_len + 1, dtype=jnp.int32)
    doc_ids = jnp.sum((starts[None, :] <= positions[:, None]).astype(jnp.int32), axis=1) - 1
    own_docs = doc_ids[1:].reshape(n, rows)
    prev = doc_ids[:-1].reshape(n, rows)[:, :1].reshape(n, 1, 1)

    vmem, anywhere = pl.BlockSpec(memory_space=pltpu.VMEM), pl.BlockSpec(memory_space=pl.ANY)
    shape = jax.ShapeDtypeStruct
    dma = pltpu.SemaphoreType.DMA
    output, end_state = pl.pallas_call(
        functools.partial(layer_kernel, n, segs),
        out_shape=(shape((rows, features), BF16), shape((heads, DK, DK), F32)),
        in_specs=[vmem] * 6 + [anywhere] * 5,
        out_specs=(vmem, vmem),
        scratch_shapes=[
            pltpu.VMEM((n, rows, features), BF16),
            pltpu.VMEM((5, features, width), BF16),
            pltpu.VMEM((n, 2, chips, piece_rows, features), BF16),
            pltpu.VMEM((n, rows, width), F32),
            pltpu.VMEM((n, rows, width), BF16),
            pltpu.VMEM((n, rows, width), BF16),
            pltpu.VMEM((n, heads, DK, DK), F32),
            pltpu.VMEM((n, 1, width), F32),
            pltpu.VMEM((segs, heads, DK + 16, DK), BF16),
            pltpu.VMEM((heads, DK, DK), F32),
            pltpu.VMEM((heads, DK, DK), F32),
            pltpu.VMEM((n, heads, DK, DK), BF16),
            pltpu.VMEM((n, rows, width), BF16),
            pltpu.VMEM((n, rows, width), BF16),
            dma((5,)), dma((2, n)), dma((n,)), dma((2, n)), dma((n,)),
            dma((n, chips)), dma((n, chips)), dma((n,)), dma((n,)),
            dma((segs,)), dma((segs,)), dma((n,)), dma((n,)),
        ],
        compiler_params=pltpu.CompilerParams(
            collective_id=0, has_side_effects=True, vmem_limit_bytes=56 * 2**20
        ),
        cost_estimate=pl.CostEstimate(
            flops=12 * seg_len * features * width, bytes_accessed=14 * features * width, transcendentals=0
        ),
        name="layer",
    )(
        tokens, decay_rate[None, :], own_docs[:, :, None], own_docs[:, None, :], prev, own_piece,
        w_query, w_key, w_value, w_gate, w_forget,
    )
    return (output, end_state[None])


def solution(mesh):
    in_specs = (
        P(("seq", "head"), None),
        P(),
        P(None, "head"),
        P(None, "head"),
        P(None, "head"),
        P(None, "head"),
        P(None, "head"),
        P("head"),
        P("head", None),
    )
    out_specs = (P(("seq", "head"), None), P("seq", "head", None, None))
    return jax.shard_map(local, mesh=mesh, in_specs=in_specs, out_specs=out_specs, check_vma=False)
```

```python
import functools

import jax
import jax.numpy as jnp
from jax import lax
from jax.experimental import pallas as pl
from jax.experimental.pallas import tpu as pltpu
from jax.sharding import PartitionSpec as P

DK = 128
PARTS = 2
MESH = pl.DeviceIdType.MESH
NT = (((1,), (1,)), ((), ()))
TN = (((0,), (0,)), ((), ()))
F32, BF16 = jnp.float32, jnp.bfloat16


def dot(a, b, dims=(((1,), (0,)), ((), ()))):
    return lax.dot_general(a, b, dims, preferred_element_type=F32)


def block_by_distance(i, z, n):
    up = jnp.where(2 * z < n, 1, -1)
    near = jnp.where(2 * z < n, z, n - 1 - z)
    half = (i + 1) // 2
    paired = jnp.where(i % 2 == 1, z + up * half, z - up * half)
    single = jnp.where(2 * z < n, i, n - 1 - i)
    return jnp.where(i <= 2 * near, paired, single)


def layer_kernel(
    n, segs, lengths_ref, tokens_ref, rate_ref, w_out, wq, wk, wv, wg, wf,
    out_ref, end_ref,
    gathered, weights, w_all, local_ref, cq_ref, gate_ref, state_ref, decay_ref,
    packets, seg_state, incoming, entering, sending, arrived,
    load_sem, piece_sem, send_sem, recv_sem, wz_send, wz_recv, wp_send, wp_recv, wc_send, wc_recv,
    state_send, state_recv, mix_send, mix_recv,
):
    z, seq = lax.axis_index("head"), lax.axis_index("seq")
    chips = segs // 2
    chip, core = seq // 2, seq % 2
    rows, features = tokens_ref.shape
    half = rows // 2
    width = rate_ref.shape[1]
    heads = width // DK
    loads = [
        pltpu.make_async_copy(w, weights.at[i], load_sem.at[i])
        for i, w in enumerate((wf, wq, wk, wv, wg))
    ]
    for load in loads:
        load.start()
    piece_rows = w_all.shape[3]
    piece_at = pl.multiple_of((core * chips + chip) * piece_rows, piece_rows)
    own_piece = pltpu.make_async_copy(
        w_out.at[pl.ds(piece_at, piece_rows), :], w_all.at[z, core, chip], piece_sem
    )
    own_piece.start()

    barrier = pltpu.get_barrier_semaphore()

    def greet_seq(away, carry):
        pl.semaphore_signal(
            barrier, inc=1, device_id={"seq": (seq + away) % segs}, device_id_type=MESH
        )
        return carry

    def greet_head(away, carry):
        pl.semaphore_signal(
            barrier, inc=1, device_id={"head": (z + away) % n}, device_id_type=MESH
        )
        return carry

    lax.fori_loop(1, segs, greet_seq, 0)
    lax.fori_loop(1, n, greet_head, 0)

    tokens = tokens_ref[...].astype(F32)
    scale = lax.rsqrt(jnp.mean(tokens * tokens, axis=-1, keepdims=True) + 1e-05)
    gathered[z] = (tokens * scale).astype(BF16)
    pl.semaphore_wait(barrier, segs - 1 + n - 1)

    def pass_tokens(b, way):
        return pltpu.make_async_remote_copy(
            src_ref=gathered.at[b],
            dst_ref=gathered.at[b],
            send_sem=send_sem.at[(way + 1) // 2, b],
            recv_sem=recv_sem.at[b],
            device_id={"head": (z + way + n) % n},
            device_id_type=MESH,
        )

    def pass_piece(b, way):
        return pltpu.make_async_remote_copy(
            src_ref=w_all.at[b, core, chip],
            dst_ref=w_all.at[b, core, chip],
            send_sem=wz_send.at[(way + 1) // 2, b],
            recv_sem=wz_recv.at[b],
            device_id={"head": (z + way + n) % n},
            device_id_type=MESH,
        )

    def spread_piece(b, source, target):
        return pltpu.make_async_remote_copy(
            src_ref=w_all.at[b, core, source],
            dst_ref=w_all.at[b, core, source],
            send_sem=wp_send.at[b, target],
            recv_sem=wp_recv.at[b, source],
            device_id={"seq": 2 * target + core},
            device_id_type=MESH,
        )

    def share_pieces(b, from_core):
        return pltpu.make_async_remote_copy(
            src_ref=w_all.at[b, from_core],
            dst_ref=w_all.at[b, from_core],
            send_sem=wc_send.at[b],
            recv_sem=wc_recv.at[b],
            device_id={"seq": 2 * chip + 1 - core},
            device_id_type=MESH,
        )

    def both_ways(b, copy, act):
        @pl.when((b <= z) & (z < n - 1))
        def _():
            act(copy(b, 1))

        @pl.when((b >= z) & (z > 0))
        def _():
            act(copy(b, -1))

    def start(copy):
        copy.start()

    def wait_send(copy):
        copy.wait_send()

    def share_after_spread(b):
        def arrival(away, carry):
            spread_piece(b, (chip + away) % chips, (chip + away) % chips).wait_recv()
            return carry

        lax.fori_loop(1, chips, arrival, 0)
        share_pieces(b, core).start()

    row_at = lax.broadcasted_iota(jnp.int32, (rows, rows), 0)
    col_at = lax.broadcasted_iota(jnp.int32, (rows, rows), 1)
    lower = row_at >= col_at
    lower_bf = lower.astype(F32).astype(BF16)

    def doc_of(position):
        doc = jnp.zeros(position.shape, jnp.int32)
        begin = jnp.int32(0)
        for j in range(lengths_ref.shape[0] - 1):
            begin = begin + lengths_ref[j]
            doc = doc + jnp.where(position >= begin, 1, 0)
        return doc

    up = jnp.where(2 * z < n, 1, -1)
    near = jnp.where(2 * z < n, z, n - 1 - z)
    far = n - 1 - near

    def spread(b):
        def one(away, carry):
            spread_piece(b, chip, (chip + away) % chips).start()
            return carry

        lax.fori_loop(1, chips, one, 0)

    def pieces_up():
        own_piece.wait()
        spread(z)

        def tokens_left(d, carry):
            pass_tokens(z - up * d, up).wait_send()
            return carry

        lax.fori_loop(0, near + 1, tokens_left, 0)
        pass_piece(z, up).start()

        def onward(d, carry):
            b = z - up * d
            pass_piece(b, up).wait_recv()
            pass_piece(b, up).start()
            spread(b)
            return carry

        lax.fori_loop(1, near + 1, onward, 0)

    def pieces_down():
        @pl.when(near > 0)
        def _():
            def tokens_left(d, carry):
                pass_tokens(z + up * d, -up).wait_send()
                return carry

            lax.fori_loop(0, far + 1, tokens_left, 0)
            pass_piece(z, -up).start()

    def piece_down(d):
        b = z + up * d
        pass_piece(b, -up).wait_recv()

        @pl.when(near > 0)
        def _():
            pass_piece(b, -up).start()

        spread(b)

    def step(i, carry):
        b = block_by_distance(i, z, n)

        @pl.when(i > 0)
        def _():
            pass_tokens(b, 1).wait_recv()

        both_ways(b, pass_tokens, start)

        @pl.when(i == jnp.where(near > 0, n - 1, 1))
        def _():
            pieces_up()

        @pl.when(i == 0)
        def _():
            for load in loads:
                load.wait()

        x = gathered[b]
        logit = dot(x, weights[0])
        softplus = jnp.maximum(logit, 0.0) + jnp.log1p(jnp.exp(-jnp.abs(logit)))
        log_decay = -rate_ref[...] * softplus
        high = log_decay.astype(BF16)
        low = (log_decay - high.astype(F32)).astype(BF16)
        cum = dot(lower_bf, high) + dot(lower_bf, low)
        q = dot(x, weights[1]).astype(BF16).astype(F32)
        k = dot(x, weights[2]).astype(BF16).astype(F32)
        v = dot(x, weights[3]).astype(BF16)
        gate_ref[b] = dot(x, weights[4]).astype(BF16)

        begin = seq * (rows * n) + b * rows
        docs = doc_of(begin + lax.broadcasted_iota(jnp.int32, (rows, 1), 0))
        docs_across = doc_of(begin + lax.broadcasted_iota(jnp.int32, (1, rows), 1))
        same = lower & (docs == docs_across)
        last_doc = docs[rows - 1 :, :]
        prev = doc_of(begin - 1 + lax.broadcasted_iota(jnp.int32, (1, 1), 0))
        carried = (docs == prev).astype(F32)
        ending = (docs == last_doc).astype(F32)
        keep = (last_doc == prev).astype(F32)
        last = cum[rows - 1 :, :]
        middle = cum[half - 1 : half, :]
        decay_ref[b] = jnp.exp(last) * keep
        cq_ref[b] = (q * jnp.exp(cum) * carried).astype(BF16)
        k_end = (k * jnp.exp(last - cum) * ending).astype(BF16)
        top, low_half = slice(0, half), slice(half, rows)
        top_mid, low_mid = 0.5 * middle, 0.5 * (middle + last)
        q_top = (q[top] * jnp.exp(cum[top] - top_mid)).astype(BF16)
        k_top = (k[top] * jnp.exp(top_mid - cum[top])).astype(BF16)
        q_low = (q[low_half] * jnp.exp(cum[low_half] - low_mid)).astype(BF16)
        k_low = (k[low_half] * jnp.exp(low_mid - cum[low_half])).astype(BF16)
        q_cross = (q[low_half] * jnp.exp(cum[low_half] - middle)).astype(BF16)
        k_cross = (k[top] * jnp.exp(middle - cum[top])).astype(BF16)
        for h in range(width // DK):
            c = slice(h * DK, (h + 1) * DK)
            s_top = jnp.where(same[top, top], dot(q_top[:, c], k_top[:, c], NT), 0.0)
            s_cross = jnp.where(same[low_half, top], dot(q_cross[:, c], k_cross[:, c], NT), 0.0)
            s_low = jnp.where(
                same[low_half, low_half], dot(q_low[:, c], k_low[:, c], NT), 0.0
            )
            local_ref[b, top, c] = dot(s_top.astype(BF16), v[top, c])
            s_both = jnp.concatenate([s_cross, s_low], axis=1).astype(BF16)
            local_ref[b, low_half, c] = dot(s_both, v[:, c])
            state_ref[b, h] = dot(v[:, c], k_end[:, c], TN)
        return carry

    lax.fori_loop(0, n, step, 0)

    per = heads // PARTS

    def send_state(part, to):
        return pltpu.make_async_remote_copy(
            src_ref=packets.at[part, seq],
            dst_ref=packets.at[part, seq],
            send_sem=state_send.at[part, to],
            recv_sem=state_recv.at[part, seq],
            device_id={"seq": to},
            device_id_type=MESH,
        )

    seg_decay = decay_ref[0]
    for b in range(1, n):
        seg_decay = seg_decay * decay_ref[b]
    high = seg_decay.astype(BF16).astype(F32)
    low = seg_decay - high
    pad_at = lax.broadcasted_iota(jnp.int32, (16, DK), 0)
    for part in range(PARTS):
        for i in range(per):
            h = part * per + i
            c = slice(h * DK, (h + 1) * DK)
            total = state_ref[0, h]
            for b in range(1, n):
                total = total * decay_ref[b][:, c] + state_ref[b, h]
            seg_state[h] = total
            packets[part, seq, i, :DK] = total.astype(BF16)
            pad = jnp.where(pad_at == 0, high[:, c], jnp.where(pad_at == 1, low[:, c], 0.0))
            packets[part, seq, i, DK:] = pad.astype(BF16)

        def send_later(away, carry):
            @pl.when(seq + away < segs)
            def _():
                send_state(part, seq + away).start()

            return carry

        lax.fori_loop(1, segs, send_later, 0)

    pieces_down()

    def early_piece(d, carry):
        piece_down(d)
        return carry

    lax.fori_loop(1, far, early_piece, 0)
    incoming[...] = jnp.zeros_like(incoming)

    def send_mix(part, b):
        return pltpu.make_async_remote_copy(
            src_ref=sending.at[part, b],
            dst_ref=arrived.at[part, z],
            send_sem=mix_send.at[part, b],
            recv_sem=mix_recv.at[part, z],
            device_id={"head": b},
            device_id_type=MESH,
        )

    for part in range(PARTS):

        def take(j, carry):
            @pl.when(j < seq)
            def _():
                pltpu.make_async_remote_copy(
                    src_ref=packets.at[part, j],
                    dst_ref=packets.at[part, j],
                    send_sem=state_send.at[part, j],
                    recv_sem=state_recv.at[part, j],
                    device_id={"seq": (seq + 1) % segs},
                    device_id_type=MESH,
                ).wait_recv()
                for i in range(per):
                    h = part * per + i
                    pad = packets[part, j, i, DK:].astype(F32)
                    decay = pad[0:1] + pad[1:2]
                    incoming[h] = incoming[h] * decay + packets[part, j, i, :DK].astype(F32)

            return carry

        lax.fori_loop(0, segs - 1, take, 0)
        for i in range(per):
            h = part * per + i
            c = slice(h * DK, (h + 1) * DK)
            held = incoming[h]
            end_ref[h] = (held * seg_decay[:, c] + seg_state[h]).T
            for b in range(n):
                entering[b, h] = held.astype(BF16)
                if b < n - 1:
                    held = held * decay_ref[b][:, c] + state_ref[b, h]

        def gated(i, carry):
            b = block_by_distance(n - 1 - i, z, n)
            for k in range(per):
                h = part * per + k
                c = slice(h * DK, (h + 1) * DK)
                mixed = local_ref[b, :, c] + dot(cq_ref[b, :, c], entering[b, h], NT)
                inverse = lax.rsqrt(jnp.mean(mixed * mixed, axis=-1, keepdims=True) + 1e-05)
                gate = gate_ref[b, :, c].astype(F32)
                result = mixed * inverse * (gate * jax.nn.sigmoid(gate))
                sending[part, b, :, k * DK : (k + 1) * DK] = result.astype(BF16)

            @pl.when(i < n - 1)
            def _():
                send_mix(part, b).start()

            return carry

        lax.fori_loop(0, n, gated, 0)
        if part == 0:
            piece_down(far)

    def share(i, carry):
        share_after_spread(block_by_distance(i, z, n))
        return carry

    lax.fori_loop(0, n, share, 0)
    wide = width // PARTS

    def whole(b):
        share_pieces(b, 1 - core).wait_recv()
        return w_all[b].reshape(width, features)

    out = tokens_ref[...].astype(F32)
    w_own = whole(z)
    for part in range(PARTS):
        out = out + dot(sending[part, z], w_own[part * wide : (part + 1) * wide])
    for away in range(1, n):
        b = block_by_distance(away, z, n)
        w_b = whole(b)
        for part in range(PARTS):
            pltpu.make_async_remote_copy(
                src_ref=sending.at[part, b],
                dst_ref=arrived.at[part, b],
                send_sem=mix_send.at[part, b],
                recv_sem=mix_recv.at[part, b],
                device_id={"head": b},
                device_id_type=MESH,
            ).wait_recv()
            out = out + dot(arrived[part, b], w_b[part * wide : (part + 1) * wide])
    out_ref[...] = out.astype(BF16)

    def finish(b, carry):
        both_ways(b, pass_piece, wait_send)
        share_pieces(b, core).wait_send()

        def spread_done(away, inner):
            spread_piece(b, chip, (chip + away) % chips).wait_send()
            return inner

        lax.fori_loop(1, chips, spread_done, 0)

        @pl.when(b != z)
        def _():
            for part in range(PARTS):
                send_mix(part, b).wait_send()

        return carry

    lax.fori_loop(0, n, finish, 0)

    def later_done(away, carry):
        @pl.when(seq + away < segs)
        def _():
            for part in range(PARTS):
                send_state(part, seq + away).wait_send()

        return carry

    lax.fori_loop(1, segs, later_done, 0)


def local(tokens, lengths, w_query, w_key, w_value, w_gate, w_forget, decay_rate, w_out):
    n, segs = lax.axis_size("head"), lax.axis_size("seq")
    rows, features = tokens.shape
    width = w_query.shape[1]
    heads = width // DK
    seg_len = rows * n
    chips = segs // 2

    piece_rows = width // segs

    vmem, anywhere = pl.BlockSpec(memory_space=pltpu.VMEM), pl.BlockSpec(memory_space=pl.ANY)
    shape = jax.ShapeDtypeStruct
    dma = pltpu.SemaphoreType.DMA
    output, end_state = pl.pallas_call(
        functools.partial(layer_kernel, n, segs),
        out_shape=(shape((rows, features), BF16), shape((heads, DK, DK), F32)),
        in_specs=[pl.BlockSpec(memory_space=pltpu.SMEM)] + [vmem] * 2 + [anywhere] * 6,
        out_specs=(vmem, vmem),
        scratch_shapes=[
            pltpu.VMEM((n, rows, features), BF16),
            pltpu.VMEM((5, features, width), BF16),
            pltpu.VMEM((n, 2, chips, piece_rows, features), BF16),
            pltpu.VMEM((n, rows, width), F32),
            pltpu.VMEM((n, rows, width), BF16),
            pltpu.VMEM((n, rows, width), BF16),
            pltpu.VMEM((n, heads, DK, DK), F32),
            pltpu.VMEM((n, 1, width), F32),
            pltpu.VMEM((PARTS, segs, heads // PARTS, DK + 16, DK), BF16),
            pltpu.VMEM((heads, DK, DK), F32),
            pltpu.VMEM((heads, DK, DK), F32),
            pltpu.VMEM((n, heads, DK, DK), BF16),
            pltpu.VMEM((PARTS, n, rows, width // PARTS), BF16),
            pltpu.VMEM((PARTS, n, rows, width // PARTS), BF16),
            dma((5,)), dma, dma((2, n)), dma((n,)), dma((2, n)), dma((n,)),
            dma((n, chips)), dma((n, chips)), dma((n,)), dma((n,)),
            dma((PARTS, segs)), dma((PARTS, segs)), dma((PARTS, n)), dma((PARTS, n)),
        ],
        compiler_params=pltpu.CompilerParams(
            collective_id=0, has_side_effects=True, vmem_limit_bytes=56 * 2**20
        ),
        cost_estimate=pl.CostEstimate(
            flops=12 * seg_len * features * width, bytes_accessed=14 * features * width, transcendentals=0
        ),
        name="layer",
    )(
        lengths, tokens, decay_rate[None, :], w_out,
        w_query, w_key, w_value, w_gate, w_forget,
    )
    return (output, end_state[None])


def solution(mesh):
    in_specs = (
        P(("seq", "head"), None),
        P(),
        P(None, "head"),
        P(None, "head"),
        P(None, "head"),
        P(None, "head"),
        P(None, "head"),
        P("head"),
        P("head", None),
    )
    out_specs = (P(("seq", "head"), None), P("seq", "head", None, None))
    return jax.shard_map(local, mesh=mesh, in_specs=in_specs, out_specs=out_specs, check_vma=False)
```
